32 devices in a mesh: row: 4 (over y, x), col: 8 (over z, core).
Axes of the slice: x: 2, y: 2, z: 4, core: 2. Of those that a mesh axis runs over, the one named last changes fastest.
Arguments:
- upper_stored: bfloat16 [3072, 3072], P('row', 'col'), may hold values from -6 to 6
- block_cells: int32 [48, 3], replicated, may hold values from 0 to 15
Outputs:
- purified: bfloat16 [3072, 3072], P('row', 'col')
The draws below stay inside these ranges and needn't reach their ends.
Inputs may be any that keep to these rules, and one draw needn't show every extreme that they name: `block_cells`: integer cell coordinates of each atom block on a periodic lattice of 16 cells a side.
All inputs are finite; a program needn't handle non-finite values.
Results may differ from the reference program's by a relative error of at most 0.0067.
Values may be sent and summed in bfloat16 or wider, within the bound.
A program may use at most 64 MiB of HBM per device.

```python
import math
import jax
import jax.numpy as jnp
from jax import lax

BLK = 64
BOX = 16
NEAR = 40
FAR = 90
NB = 48
N = 3072


def touch_ends(entries, stream_key, low, largest):
    dims = entries.shape
    place = [jax.random.randint(jax.random.fold_in(stream_key, axis), (), 0, dims[axis]) for axis in range(len(dims))]
    entries = entries.at[tuple(place)].set(low)
    longest = dims.index(max(dims))
    place[longest] = (place[longest] + 1) % dims[longest]
    return entries.at[tuple(place)].set(largest)


def block_scale(stream_key, dims, cuts, least, top_value):
    def one(position, blocks):
        draws = jax.random.uniform(jax.random.fold_in(jax.random.fold_in(stream_key, 6), position), (blocks,), jnp.float32, least / len(cuts), top_value / len(cuts))
        return jnp.repeat(jnp.exp(draws), dims[position] // blocks).reshape((-1,) + (1,) * (len(dims) - position - 1))

    gain = one(*cuts[0])
    for cut in cuts[1:]:
        gain = gain * one(*cut)
    return gain


def scatter_about(rng, extent, scale, reach, split=(), kind=jnp.bfloat16):
    array = scale * jax.random.normal(rng, extent, jnp.float32)
    if split:
        array = array * block_scale(rng, extent, split, -0.22, 0.18)
    return jnp.clip(array, -reach, reach).astype(kind)


def setup_inputs(seed: int = 0) -> dict:
    splits = jax.random.split(jax.random.key(seed), 3)
    return {
        "upper_stored": scatter_about(splits[0], (N, N), 1.0, 6.0, ((0, 4), (1, 8))),
        "block_cells": touch_ends(jax.random.randint(splits[1], (NB, 3), 0, BOX), jax.random.fold_in(splits[1], 1), 0, BOX - 1).astype(jnp.int32),
    }


def cell_mask(block_cells, bound_sq):
    offset_abs = jnp.abs(block_cells[:, None, :] - block_cells[None, :, :])
    wrapped = jnp.minimum(offset_abs, BOX - offset_abs)
    return lax.optimization_barrier(jnp.sum(wrapped * wrapped, axis=2)) <= bound_sq

def expand_mask(keep_mask):
    return jnp.repeat(jnp.repeat(keep_mask, BLK, axis=0), BLK, axis=1)

def reference(upper_stored, block_cells):
    order_total = upper_stored.shape[0]
    index_rows = lax.broadcasted_iota(jnp.int32, (order_total, order_total), 0)
    index_cols = lax.broadcasted_iota(jnp.int32, (order_total, order_total), 1)
    symmetric = jnp.where(index_rows <= index_cols, upper_stored, upper_stored.T)
    near_keep = expand_mask(cell_mask(block_cells, NEAR))
    far_keep = expand_mask(cell_mask(block_cells, FAR))
    diagonal = jnp.where(index_rows == index_cols, 0.5, 0.0).astype(jnp.float32)
    value_scale = 2.0 / math.sqrt(order_total)
    density_full = diagonal + value_scale * symmetric.astype(jnp.float32)
    density = jnp.where(near_keep, density_full, jnp.zeros_like(density_full)).astype(jnp.bfloat16)
    product = jnp.dot(density, density, preferred_element_type=jnp.float32)
    square = jnp.where(far_keep, product, jnp.zeros_like(product))
    square_low = square.astype(jnp.bfloat16)
    cubic = jnp.dot(square_low, density, preferred_element_type=jnp.float32)
    result = 3.0 * square - 2.0 * cubic
    return jnp.where(near_keep, result, jnp.zeros_like(result)).astype(jnp.bfloat16)
```

```python
import math

import jax
import jax.numpy as jnp
from jax import lax
from jax.sharding import PartitionSpec as P

BLK = 64
BOX = 16
NEAR = 40
FAR = 90


def shifted_2(array, axis, by):
    length = lax.axis_size(axis)
    return lax.ppermute(array, axis, [(i, (i + by) % length) for i in range(length)])


def partner(value, axis, bit):
    mask = 2**bit
    pairs = [(source, source ^ mask) for source in range(lax.axis_size(axis))]
    return lax.ppermute(value, axis, pairs)


def cell_mask(block_cells, row_start, row_count, col_start, col_count, bound_sq):
    row_cells = lax.dynamic_slice_in_dim(block_cells, row_start, row_count, 0)
    col_cells = lax.dynamic_slice_in_dim(block_cells, col_start, col_count, 0)
    offset_abs = jnp.abs(row_cells[:, None, :] - col_cells[None, :, :])
    wrapped = jnp.minimum(offset_abs, BOX - offset_abs)
    return jnp.sum(wrapped * wrapped, axis=2) <= bound_sq


def block_keep(matrix_tile, keep_mask):
    row_count, col_count = matrix_tile.shape
    row_blocks, col_blocks = keep_mask.shape
    shaped = matrix_tile.reshape(
        row_blocks, row_count // row_blocks, col_blocks, col_count // col_blocks
    )
    kept = jnp.where(keep_mask[:, None, :, None], shaped, jnp.zeros_like(shaped))
    return kept.reshape(row_count, col_count)


def own_part(matrix_tile, layer_bit, half_width):
    return jnp.where(layer_bit == 0, matrix_tile[:, :half_width], matrix_tile[:, half_width:])


def partner_part(matrix_tile, layer_bit, half_width):
    return jnp.where(layer_bit == 0, matrix_tile[:, half_width:], matrix_tile[:, :half_width])


def join_halves(own_piece, partner_piece, layer_bit):
    first_order = jnp.concatenate([own_piece, partner_piece], 1)
    second_order = jnp.concatenate([partner_piece, own_piece], 1)
    return jnp.where(layer_bit == 0, first_order, second_order)


def skew_left(operand, row_id, layer_bit, grid_size):
    steps_wanted = (row_id + layer_bit * (grid_size // 2)) % grid_size
    for bit_pos in range((grid_size - 1).bit_length()):
        shifted = shifted_2(operand, "col", -(2 << bit_pos))
        operand = jnp.where((steps_wanted >> bit_pos) % 2 == 1, shifted, operand)
    return operand


def skew_right(operand, tile_col, layer_bit, grid_size):
    steps_wanted = (tile_col + layer_bit * (grid_size // 2)) % grid_size
    for bit_pos in range((grid_size - 1).bit_length()):
        shifted = shifted_2(operand, "row", -(1 << bit_pos))
        operand = jnp.where((steps_wanted >> bit_pos) % 2 == 1, shifted, operand)
    return operand


def cannon_half(left, right, grid_size):
    running = jnp.zeros((left.shape[0], right.shape[1]), jnp.float32)
    for section in range(grid_size // 2):
        running = running + jnp.dot(left, right, preferred_element_type=jnp.float32)
        if section + 1 < grid_size // 2:
            left = shifted_2(left, "col", -2)
            right = shifted_2(right, "row", -1)
    return running


def per_device_ring(upper_stored, block_cells):
    grid_size = lax.axis_size("row")
    row_id = lax.axis_index("row")
    col_id = lax.axis_index("col")
    layer_bit = col_id % 2
    tile_col = col_id // 2
    tile_side, half_width = upper_stored.shape
    order_total = tile_side * grid_size
    tile_blocks = tile_side // BLK
    half_blocks = half_width // BLK
    slab_width = half_width // grid_size
    stacked = lax.all_to_all(
        lax.all_to_all(upper_stored, "row", split_axis=1, concat_axis=0, tiled=True),
        "col",
        split_axis=0,
        concat_axis=1,
        tiled=True,
    )
    gathered = lax.all_to_all(stacked.T, "row", split_axis=0, concat_axis=0, tiled=True)
    mirrored = (
        gathered.reshape(grid_size, 2, slab_width, half_width)
        .transpose(1, 0, 2, 3)
        .reshape(tile_side, half_width)
    )
    global_rows = row_id * tile_side + lax.broadcasted_iota(jnp.int32, (tile_side, half_width), 0)
    global_cols = col_id * half_width + lax.broadcasted_iota(jnp.int32, (tile_side, half_width), 1)
    symmetric = jnp.where(global_rows <= global_cols, upper_stored, mirrored)
    near_own = cell_mask(
        block_cells, row_id * tile_blocks, tile_blocks, col_id * half_blocks, half_blocks, NEAR
    )
    diagonal = jnp.where(global_rows == global_cols, 0.5, 0.0).astype(jnp.float32)
    value_scale = 2.0 / math.sqrt(order_total)
    own_density = block_keep(
        diagonal + value_scale * symmetric.astype(jnp.float32), near_own
    ).astype(jnp.bfloat16)
    partner_density = partner(own_density, "col", 0)
    density = join_halves(own_density, partner_density, layer_bit)
    right_start = skew_right(density, tile_col, layer_bit, grid_size)
    left_start = skew_left(density, row_id, layer_bit, grid_size)
    running = cannon_half(left_start, right_start, grid_size)
    far_full = cell_mask(
        block_cells, row_id * tile_blocks, tile_blocks, tile_col * tile_blocks, tile_blocks, FAR
    )
    partner_running = partner(running, "col", 0)
    square = block_keep(running + partner_running, far_full)
    square_low = square.astype(jnp.bfloat16)
    own_square = own_part(square, layer_bit, half_width)
    right_again = skew_right(density, tile_col, layer_bit, grid_size)
    left_again = skew_left(square_low, row_id, layer_bit, grid_size)
    cubic_running = cannon_half(left_again, right_again, grid_size)
    received_cubic = partner(partner_part(cubic_running, layer_bit, half_width), "col", 0)
    cubic = own_part(cubic_running, layer_bit, half_width) + received_cubic
    return block_keep(3.0 * own_square - 2.0 * cubic, near_own).astype(jnp.bfloat16)


def per_device_gather(upper_stored, block_cells):
    row_id = lax.axis_index("row")
    col_id = lax.axis_index("col")
    rows, cols = upper_stored.shape
    order_total = rows * lax.axis_size("row")
    row_blocks, col_blocks = rows // BLK, cols // BLK
    all_blocks = order_total // BLK
    near_own = cell_mask(
        block_cells, row_id * row_blocks, row_blocks, col_id * col_blocks, col_blocks, NEAR
    )
    global_rows = row_id * rows + lax.broadcasted_iota(jnp.int32, (rows, cols), 0)
    global_cols = col_id * cols + lax.broadcasted_iota(jnp.int32, (rows, cols), 1)
    diagonal = jnp.where(global_rows == global_cols, 0.5, 0.0).astype(jnp.float32)
    value_scale = 2.0 / math.sqrt(order_total)
    own_upper = block_keep(
        diagonal + value_scale * upper_stored.astype(jnp.float32), near_own
    ).astype(jnp.bfloat16)
    blocks = lax.all_gather(own_upper, ("row", "col"))
    grid = blocks.reshape(lax.axis_size("row"), lax.axis_size("col"), rows, cols)
    upper = grid.transpose(0, 2, 1, 3).reshape(order_total, order_total)
    i0 = lax.broadcasted_iota(jnp.int32, (order_total, order_total), 0)
    i1 = lax.broadcasted_iota(jnp.int32, (order_total, order_total), 1)
    density = jnp.where(i0 <= i1, upper, upper.T)
    left = lax.dynamic_slice_in_dim(density, row_id * rows, rows, 0)
    right = lax.dynamic_slice_in_dim(density, col_id * cols, cols, 1)
    far = cell_mask(block_cells, row_id * row_blocks, row_blocks, 0, all_blocks, FAR)
    square = block_keep(jnp.dot(left, density, preferred_element_type=jnp.float32), far)
    square_low = square.astype(jnp.bfloat16)
    own_square = lax.dynamic_slice_in_dim(square, col_id * cols, cols, 1)
    cubic = jnp.dot(square_low, right, preferred_element_type=jnp.float32)
    return block_keep(3.0 * own_square - 2.0 * cubic, near_own).astype(jnp.bfloat16)


def per_device(upper_stored, block_cells):
    order_total = upper_stored.shape[0] * lax.axis_size("row")
    if order_total * order_total * 2 > 24 * 2**20:
        return per_device_ring(upper_stored, block_cells)
    return per_device_gather(upper_stored, block_cells)


def solution(mesh):
    return jax.shard_map(
        per_device,
        mesh=mesh,
        in_specs=(P("row", "col"), P()),
        out_specs=P("row", "col"),
        check_vma=False,
    )
```

```python
import math

import jax
import jax.numpy as jnp
from jax import lax
from jax.experimental import pallas as pl
from jax.experimental.pallas import tpu as pltpu
from jax.sharding import PartitionSpec as P

BLK = 64
BOX = 16
NEAR = 40
FAR = 90


def shifted_2(array, axis, by):
    length = lax.axis_size(axis)
    return lax.ppermute(array, axis, [(i, (i + by) % length) for i in range(length)])


def partner(value, axis, bit):
    mask = 2**bit
    pairs = [(source, source ^ mask) for source in range(lax.axis_size(axis))]
    return lax.ppermute(value, axis, pairs)


def cell_mask(block_cells, row_start, row_count, col_start, col_count, bound_sq):
    row_cells = lax.dynamic_slice_in_dim(block_cells, row_start, row_count, 0)
    col_cells = lax.dynamic_slice_in_dim(block_cells, col_start, col_count, 0)
    offset_abs = jnp.abs(row_cells[:, None, :] - col_cells[None, :, :])
    wrapped = jnp.minimum(offset_abs, BOX - offset_abs)
    return jnp.sum(wrapped * wrapped, axis=2) <= bound_sq


def block_keep(matrix_tile, keep_mask):
    row_count, col_count = matrix_tile.shape
    row_blocks, col_blocks = keep_mask.shape
    shaped = matrix_tile.reshape(
        row_blocks, row_count // row_blocks, col_blocks, col_count // col_blocks
    )
    kept = jnp.where(keep_mask[:, None, :, None], shaped, jnp.zeros_like(shaped))
    return kept.reshape(row_count, col_count)


def own_part(matrix_tile, layer_bit, half_width):
    return jnp.where(layer_bit == 0, matrix_tile[:, :half_width], matrix_tile[:, half_width:])


def partner_part(matrix_tile, layer_bit, half_width):
    return jnp.where(layer_bit == 0, matrix_tile[:, half_width:], matrix_tile[:, :half_width])


def join_halves(own_piece, partner_piece, layer_bit):
    first_order = jnp.concatenate([own_piece, partner_piece], 1)
    second_order = jnp.concatenate([partner_piece, own_piece], 1)
    return jnp.where(layer_bit == 0, first_order, second_order)


def skew_left(operand, row_id, layer_bit, grid_size):
    steps_wanted = (row_id + layer_bit * (grid_size // 2)) % grid_size
    for bit_pos in range((grid_size - 1).bit_length()):
        shifted = shifted_2(operand, "col", -(2 << bit_pos))
        operand = jnp.where((steps_wanted >> bit_pos) % 2 == 1, shifted, operand)
    return operand


def skew_right(operand, tile_col, layer_bit, grid_size):
    steps_wanted = (tile_col + layer_bit * (grid_size // 2)) % grid_size
    for bit_pos in range((grid_size - 1).bit_length()):
        shifted = shifted_2(operand, "row", -(1 << bit_pos))
        operand = jnp.where((steps_wanted >> bit_pos) % 2 == 1, shifted, operand)
    return operand


def cannon_half(left, right, grid_size):
    running = jnp.zeros((left.shape[0], right.shape[1]), jnp.float32)
    for section in range(grid_size // 2):
        running = running + jnp.dot(left, right, preferred_element_type=jnp.float32)
        if section + 1 < grid_size // 2:
            left = shifted_2(left, "col", -2)
            right = shifted_2(right, "row", -1)
    return running


def per_device_ring(upper_stored, block_cells):
    grid_size = lax.axis_size("row")
    row_id = lax.axis_index("row")
    col_id = lax.axis_index("col")
    layer_bit = col_id % 2
    tile_col = col_id // 2
    tile_side, half_width = upper_stored.shape
    order_total = tile_side * grid_size
    tile_blocks = tile_side // BLK
    half_blocks = half_width // BLK
    slab_width = half_width // grid_size
    stacked = lax.all_to_all(
        lax.all_to_all(upper_stored, "row", split_axis=1, concat_axis=0, tiled=True),
        "col",
        split_axis=0,
        concat_axis=1,
        tiled=True,
    )
    gathered = lax.all_to_all(stacked.T, "row", split_axis=0, concat_axis=0, tiled=True)
    mirrored = (
        gathered.reshape(grid_size, 2, slab_width, half_width)
        .transpose(1, 0, 2, 3)
        .reshape(tile_side, half_width)
    )
    global_rows = row_id * tile_side + lax.broadcasted_iota(jnp.int32, (tile_side, half_width), 0)
    global_cols = col_id * half_width + lax.broadcasted_iota(jnp.int32, (tile_side, half_width), 1)
    symmetric = jnp.where(global_rows <= global_cols, upper_stored, mirrored)
    near_own = cell_mask(
        block_cells, row_id * tile_blocks, tile_blocks, col_id * half_blocks, half_blocks, NEAR
    )
    diagonal = jnp.where(global_rows == global_cols, 0.5, 0.0).astype(jnp.float32)
    value_scale = 2.0 / math.sqrt(order_total)
    own_density = block_keep(
        diagonal + value_scale * symmetric.astype(jnp.float32), near_own
    ).astype(jnp.bfloat16)
    partner_density = partner(own_density, "col", 0)
    density = join_halves(own_density, partner_density, layer_bit)
    right_start = skew_right(density, tile_col, layer_bit, grid_size)
    left_start = skew_left(density, row_id, layer_bit, grid_size)
    running = cannon_half(left_start, right_start, grid_size)
    far_full = cell_mask(
        block_cells, row_id * tile_blocks, tile_blocks, tile_col * tile_blocks, tile_blocks, FAR
    )
    partner_running = partner(running, "col", 0)
    square = block_keep(running + partner_running, far_full)
    square_low = square.astype(jnp.bfloat16)
    own_square = own_part(square, layer_bit, half_width)
    right_again = skew_right(density, tile_col, layer_bit, grid_size)
    left_again = skew_left(square_low, row_id, layer_bit, grid_size)
    cubic_running = cannon_half(left_again, right_again, grid_size)
    received_cubic = partner(partner_part(cubic_running, layer_bit, half_width), "col", 0)
    cubic = own_part(cubic_running, layer_bit, half_width) + received_cubic
    return block_keep(3.0 * own_square - 2.0 * cubic, near_own).astype(jnp.bfloat16)


def wrapped_square(row_cells, col_cells):
    total = 0
    for axis in range(3):
        offset = jnp.abs(row_cells[axis] - col_cells[axis])
        wrapped = jnp.minimum(offset, BOX - offset)
        total = total + wrapped * wrapped
    return total


def masked_density(upper_stored, block_cells):
    rows, cols = upper_stored.shape
    row_start = lax.axis_index("row") * rows
    col_start = lax.axis_index("col") * cols
    order_total = rows * lax.axis_size("row")
    row_cells = lax.dynamic_slice_in_dim(block_cells, row_start // BLK, rows // BLK, 0)
    col_cells = lax.dynamic_slice_in_dim(block_cells, col_start // BLK, cols // BLK, 0)
    row_cells = jnp.repeat(row_cells, BLK, axis=0)
    col_cells = jnp.repeat(col_cells, BLK, axis=0)
    near = wrapped_square(
        [row_cells[:, a][:, None] for a in range(3)], [col_cells[:, a][None, :] for a in range(3)]
    )
    global_rows = row_start + lax.broadcasted_iota(jnp.int32, (rows, cols), 0)
    global_cols = col_start + lax.broadcasted_iota(jnp.int32, (rows, cols), 1)
    diagonal = jnp.where(global_rows == global_cols, 0.5, 0.0).astype(jnp.float32)
    value = diagonal + (2.0 / math.sqrt(order_total)) * upper_stored.astype(jnp.float32)
    return jnp.where(near <= NEAR, value, 0.0).astype(jnp.bfloat16)


def purify_kernel(cells_ref, lanes_ref, blocks_ref, out_ref, density, square_low, own, sems):
    rows, cols = out_ref.shape
    order_total = density.shape[0]
    columns = order_total // cols
    per_row = rows // cols
    row_id = lax.axis_index("row")
    col_id = lax.axis_index("col")

    def load(i, j):
        return pltpu.make_async_copy(
            blocks_ref.at[(i // per_row) * columns + j, pl.ds((i % per_row) * cols, cols)],
            density.at[pl.ds(i * cols, cols), pl.ds(j * cols, cols)],
            sems.at[i * columns + j],
        )

    pairs = [(i, j) for j in range(columns) for i in range(j + 1)]
    for i, j in pairs:
        load(i, j).start()
    below = lax.broadcasted_iota(jnp.int32, (cols, cols), 0) > lax.broadcasted_iota(
        jnp.int32, (cols, cols), 1
    )
    for i, j in pairs:
        load(i, j).wait()
        upper = density[i * cols : (i + 1) * cols, j * cols : (j + 1) * cols]
        flipped = upper.T
        if i == j:
            flipped = jnp.where(below, flipped, upper)
        density[j * cols : (j + 1) * cols, i * cols : (i + 1) * cols] = flipped

    def keep(value, lanes, bound):
        pieces = []
        for block in range(rows // BLK):
            row = row_id * (rows // BLK) + block
            distance = wrapped_square(
                [cells_ref[row, a] for a in range(3)], [lanes[a : a + 1, :] for a in range(3)]
            )
            piece = value[block * BLK : (block + 1) * BLK]
            pieces.append(jnp.where(distance <= bound, piece, 0.0))
        return jnp.concatenate(pieces, 0)

    own_rows = pl.ds(pl.multiple_of(row_id * rows, rows), rows)

    @pl.loop(0, columns)
    def _(j):
        here = pl.ds(pl.multiple_of(j * cols, cols), cols)
        product = jnp.dot(
            density[own_rows, :], density[:, here], preferred_element_type=jnp.float32
        )
        square = keep(product, lanes_ref[:, here], FAR)
        square_low[:, here] = square.astype(jnp.bfloat16)

        @pl.when(j == col_id)
        def _():
            own[...] = square

    mine = pl.ds(pl.multiple_of(col_id * cols, cols), cols)
    cubic = jnp.dot(square_low[...], density[:, mine], preferred_element_type=jnp.float32)
    result = 3.0 * own[...] - 2.0 * cubic
    out_ref[...] = keep(result, lanes_ref[:, mine], NEAR).astype(jnp.bfloat16)


def per_device_gather(upper_stored, block_cells):
    rows, cols = upper_stored.shape
    order_total = rows * lax.axis_size("row")
    columns = order_total // cols
    blocks = lax.all_gather(masked_density(upper_stored, block_cells), ("row", "col"))
    lanes = jnp.zeros((8, order_total), jnp.int32).at[:3].set(jnp.repeat(block_cells, BLK, axis=0).T)
    vmem = pl.BlockSpec(memory_space=pltpu.VMEM)
    return pl.pallas_call(
        purify_kernel,
        out_shape=jax.ShapeDtypeStruct((rows, cols), jnp.bfloat16),
        in_specs=[
            pl.BlockSpec(memory_space=pltpu.SMEM),
            vmem,
            pl.BlockSpec(memory_space=pl.ANY),
        ],
        out_specs=vmem,
        scratch_shapes=[
            pltpu.VMEM((order_total, order_total), jnp.bfloat16),
            pltpu.VMEM((rows, order_total), jnp.bfloat16),
            pltpu.VMEM((rows, cols), jnp.float32),
            pltpu.SemaphoreType.DMA((columns * columns,)),
        ],
        compiler_params=pltpu.CompilerParams(vmem_limit_bytes=48 * 2**20),
    )(block_cells, lanes, blocks)


def per_device(upper_stored, block_cells):
    order_total = upper_stored.shape[0] * lax.axis_size("row")
    if order_total * order_total * 2 > 24 * 2**20:
        return per_device_ring(upper_stored, block_cells)
    return per_device_gather(upper_stored, block_cells)


def solution(mesh):
    return jax.shard_map(
        per_device,
        mesh=mesh,
        in_specs=(P("row", "col"), P()),
        out_specs=P("row", "col"),
        check_vma=False,
    )
```

```python
import math

import jax
import jax.numpy as jnp
from jax import lax
from jax.experimental import pallas as pl
from jax.experimental.pallas import tpu as pltpu
from jax.sharding import PartitionSpec as P

BLK = 64
BOX = 16
NEAR = 40
FAR = 90


def shifted_2(array, axis, by):
    length = lax.axis_size(axis)
    return lax.ppermute(array, axis, [(i, (i + by) % length) for i in range(length)])


def partner(value, axis, bit):
    mask = 2**bit
    pairs = [(source, source ^ mask) for source in range(lax.axis_size(axis))]
    return lax.ppermute(value, axis, pairs)


def cell_mask(block_cells, row_start, row_count, col_start, col_count, bound_sq):
    row_cells = lax.dynamic_slice_in_dim(block_cells, row_start, row_count, 0)
    col_cells = lax.dynamic_slice_in_dim(block_cells, col_start, col_count, 0)
    offset_abs = jnp.abs(row_cells[:, None, :] - col_cells[None, :, :])
    wrapped = jnp.minimum(offset_abs, BOX - offset_abs)
    return jnp.sum(wrapped * wrapped, axis=2) <= bound_sq


def block_keep(matrix_tile, keep_mask):
    row_count, col_count = matrix_tile.shape
    row_blocks, col_blocks = keep_mask.shape
    shaped = matrix_tile.reshape(
        row_blocks, row_count // row_blocks, col_blocks, col_count // col_blocks
    )
    kept = jnp.where(keep_mask[:, None, :, None], shaped, jnp.zeros_like(shaped))
    return kept.reshape(row_count, col_count)


def own_part(matrix_tile, layer_bit, half_width):
    return jnp.where(layer_bit == 0, matrix_tile[:, :half_width], matrix_tile[:, half_width:])


def partner_part(matrix_tile, layer_bit, half_width):
    return jnp.where(layer_bit == 0, matrix_tile[:, half_width:], matrix_tile[:, :half_width])


def join_halves(own_piece, partner_piece, layer_bit):
    first_order = jnp.concatenate([own_piece, partner_piece], 1)
    second_order = jnp.concatenate([partner_piece, own_piece], 1)
    return jnp.where(layer_bit == 0, first_order, second_order)


def skew_left(operand, row_id, layer_bit, grid_size):
    steps_wanted = (row_id + layer_bit * (grid_size // 2)) % grid_size
    for bit_pos in range((grid_size - 1).bit_length()):
        shifted = shifted_2(operand, "col", -(2 << bit_pos))
        operand = jnp.where((steps_wanted >> bit_pos) % 2 == 1, shifted, operand)
    return operand


def skew_right(operand, tile_col, layer_bit, grid_size):
    steps_wanted = (tile_col + layer_bit * (grid_size // 2)) % grid_size
    for bit_pos in range((grid_size - 1).bit_length()):
        shifted = shifted_2(operand, "row", -(1 << bit_pos))
        operand = jnp.where((steps_wanted >> bit_pos) % 2 == 1, shifted, operand)
    return operand


def cannon_half(left, right, grid_size):
    running = jnp.zeros((left.shape[0], right.shape[1]), jnp.float32)
    for section in range(grid_size // 2):
        running = running + jnp.dot(left, right, preferred_element_type=jnp.float32)
        if section + 1 < grid_size // 2:
            left = shifted_2(left, "col", -2)
            right = shifted_2(right, "row", -1)
    return running


def per_device_ring(upper_stored, block_cells):
    grid_size = lax.axis_size("row")
    row_id = lax.axis_index("row")
    col_id = lax.axis_index("col")
    layer_bit = col_id % 2
    tile_col = col_id // 2
    tile_side, half_width = upper_stored.shape
    order_total = tile_side * grid_size
    tile_blocks = tile_side // BLK
    half_blocks = half_width // BLK
    slab_width = half_width // grid_size
    stacked = lax.all_to_all(
        lax.all_to_all(upper_stored, "row", split_axis=1, concat_axis=0, tiled=True),
        "col",
        split_axis=0,
        concat_axis=1,
        tiled=True,
    )
    gathered = lax.all_to_all(stacked.T, "row", split_axis=0, concat_axis=0, tiled=True)
    mirrored = (
        gathered.reshape(grid_size, 2, slab_width, half_width)
        .transpose(1, 0, 2, 3)
        .reshape(tile_side, half_width)
    )
    global_rows = row_id * tile_side + lax.broadcasted_iota(jnp.int32, (tile_side, half_width), 0)
    global_cols = col_id * half_width + lax.broadcasted_iota(jnp.int32, (tile_side, half_width), 1)
    symmetric = jnp.where(global_rows <= global_cols, upper_stored, mirrored)
    near_own = cell_mask(
        block_cells, row_id * tile_blocks, tile_blocks, col_id * half_blocks, half_blocks, NEAR
    )
    diagonal = jnp.where(global_rows == global_cols, 0.5, 0.0).astype(jnp.float32)
    value_scale = 2.0 / math.sqrt(order_total)
    own_density = block_keep(
        diagonal + value_scale * symmetric.astype(jnp.float32), near_own
    ).astype(jnp.bfloat16)
    partner_density = partner(own_density, "col", 0)
    density = join_halves(own_density, partner_density, layer_bit)
    right_start = skew_right(density, tile_col, layer_bit, grid_size)
    left_start = skew_left(density, row_id, layer_bit, grid_size)
    running = cannon_half(left_start, right_start, grid_size)
    far_full = cell_mask(
        block_cells, row_id * tile_blocks, tile_blocks, tile_col * tile_blocks, tile_blocks, FAR
    )
    partner_running = partner(running, "col", 0)
    square = block_keep(running + partner_running, far_full)
    square_low = square.astype(jnp.bfloat16)
    own_square = own_part(square, layer_bit, half_width)
    right_again = skew_right(density, tile_col, layer_bit, grid_size)
    left_again = skew_left(square_low, row_id, layer_bit, grid_size)
    cubic_running = cannon_half(left_again, right_again, grid_size)
    received_cubic = partner(partner_part(cubic_running, layer_bit, half_width), "col", 0)
    cubic = own_part(cubic_running, layer_bit, half_width) + received_cubic
    return block_keep(3.0 * own_square - 2.0 * cubic, near_own).astype(jnp.bfloat16)


def wrapped_square(row_cells, col_cells):
    total = 0
    for axis in range(3):
        offset = jnp.abs(row_cells[axis] - col_cells[axis])
        wrapped = jnp.minimum(offset, BOX - offset)
        total = total + wrapped * wrapped
    return total


def masked_density(upper_stored, block_cells):
    rows, cols = upper_stored.shape
    row_start = lax.axis_index("row") * rows
    col_start = lax.axis_index("col") * cols
    order_total = rows * lax.axis_size("row")
    row_cells = lax.dynamic_slice_in_dim(block_cells, row_start // BLK, rows // BLK, 0)
    col_cells = lax.dynamic_slice_in_dim(block_cells, col_start // BLK, cols // BLK, 0)
    row_cells = jnp.repeat(row_cells, BLK, axis=0)
    col_cells = jnp.repeat(col_cells, BLK, axis=0)
    near = wrapped_square(
        [row_cells[:, a][:, None] for a in range(3)], [col_cells[:, a][None, :] for a in range(3)]
    )
    global_rows = row_start + lax.broadcasted_iota(jnp.int32, (rows, cols), 0)
    global_cols = col_start + lax.broadcasted_iota(jnp.int32, (rows, cols), 1)
    diagonal = jnp.where(global_rows == global_cols, 0.5, 0.0).astype(jnp.float32)
    value = diagonal + (2.0 / math.sqrt(order_total)) * upper_stored.astype(jnp.float32)
    return jnp.where(near <= NEAR, value, 0.0).astype(jnp.bfloat16)


def purify_kernel(cells_ref, lanes_ref, blocks_ref, out_ref, density, square_low, own, sems):
    rows, cols = out_ref.shape
    order_total = density.shape[0]
    columns = order_total // cols
    per_row = rows // cols
    row_id = lax.axis_index("row")
    col_id = lax.axis_index("col")

    def load(i, j):
        return pltpu.make_async_copy(
            blocks_ref.at[(i // per_row) * columns + j, pl.ds((i % per_row) * cols, cols)],
            density.at[pl.ds(i * cols, cols), pl.ds(j * cols, cols)],
            sems.at[i * columns + j],
        )

    pairs = [(i, j) for j in range(columns) for i in range(j + 1)]
    for i, j in pairs:
        load(i, j).start()
    below = lax.broadcasted_iota(jnp.int32, (cols, cols), 0) > lax.broadcasted_iota(
        jnp.int32, (cols, cols), 1
    )
    for i, j in pairs:
        load(i, j).wait()
        upper = density[i * cols : (i + 1) * cols, j * cols : (j + 1) * cols]
        flipped = upper.T
        if i == j:
            flipped = jnp.where(below, flipped, upper)
        density[j * cols : (j + 1) * cols, i * cols : (i + 1) * cols] = flipped

    def keep(value, lanes, bound):
        pieces = []
        for block in range(rows // BLK):
            row = row_id * (rows // BLK) + block
            distance = wrapped_square(
                [cells_ref[row, a] for a in range(3)], [lanes[a : a + 1, :] for a in range(3)]
            )
            piece = value[block * BLK : (block + 1) * BLK]
            pieces.append(jnp.where(distance <= bound, piece, 0.0))
        return jnp.concatenate(pieces, 0)

    own_rows = pl.ds(pl.multiple_of(row_id * rows, rows), rows)

    @pl.loop(0, columns)
    def _(j):
        here = pl.ds(pl.multiple_of(j * cols, cols), cols)
        product = jnp.dot(
            density[own_rows, :], density[:, here], preferred_element_type=jnp.float32
        )
        square = keep(product, lanes_ref[:, here], FAR)
        square_low[:, here] = square.astype(jnp.bfloat16)

        @pl.when(j == col_id)
        def _():
            own[...] = square

    mine = pl.ds(pl.multiple_of(col_id * cols, cols), cols)
    cubic = jnp.dot(square_low[...], density[:, mine], preferred_element_type=jnp.float32)
    result = 3.0 * own[...] - 2.0 * cubic
    out_ref[...] = keep(result, lanes_ref[:, mine], NEAR).astype(jnp.bfloat16)


def gather_kernel(
    own_ref, blocks_ref, z_send, z_recv, p_send, p_recv, d_send, d_recv, c_send, c_recv, local_sem
):
    rows = own_ref.shape[0]
    half = rows // 2
    columns = lax.axis_size("col")
    layers = columns // 2
    row_id = lax.axis_index("row")
    col_id = lax.axis_index("col")
    z, core = col_id // 2, col_id % 2
    x_row = row_id + 1 - 2 * (row_id % 2)
    y_row = (row_id + 2) % 4
    diag_row = (x_row + 2) % 4
    mesh_id = pl.DeviceIdType.MESH
    to_x, to_y = (x_row, col_id), (y_row, col_id)
    to_core = (row_id, col_id + 1 - 2 * core)
    up, down = (row_id, col_id + 2), (row_id, col_id - 2)
    has_up, has_down = z + 1 < layers, z > 0

    barrier = pltpu.get_barrier_semaphore()
    for target in (to_x, to_y, to_core):
        pl.semaphore_signal(barrier, inc=1, device_id=target, device_id_type=mesh_id)

    @pl.when(has_up)
    def _():
        pl.semaphore_signal(barrier, inc=1, device_id=up, device_id_type=mesh_id)

    @pl.when(has_down)
    def _():
        pl.semaphore_signal(barrier, inc=1, device_id=down, device_id_type=mesh_id)

    pl.semaphore_wait(barrier, 3 + has_up.astype(jnp.int32) + has_down.astype(jnp.int32))

    far_slot = layers - 1
    slots = [0]
    for step in range(far_slot):
        slots += [1 + step, 1 + far_slot + step]

    def layer(slot):
        if slot == 0:
            return z
        if slot <= far_slot:
            return z - slot
        return z + slot - far_slot

    def valid(slot, act):
        if slot == 0:
            act()
        elif slot <= far_slot:
            pl.when(z >= slot)(act)
        else:
            pl.when(z + slot - far_slot < layers)(act)

    def part(row, slot, piece):
        index = row * columns + 2 * layer(slot) + core
        block = blocks_ref.at[index]
        return block if piece is None else block.at[pl.ds(piece * half, half)]

    def copy(row, slot, piece, target, send, recv, first=False):
        place = part(row, slot, piece)
        return pltpu.make_async_remote_copy(
            src_ref=own_ref if first else place,
            dst_ref=place,
            send_sem=send,
            recv_sem=recv,
            device_id=target,
            device_id_type=mesh_id,
        )

    def z_up(slot):
        return copy(row_id, slot, None, up, z_send.at[slot, 0], z_recv.at[slot + 1], slot == 0)

    def z_down(slot):
        later = 1 + far_slot if slot == 0 else slot + 1
        return copy(row_id, slot, None, down, z_send.at[slot, 1], z_recv.at[later], slot == 0)

    def goes_up(slot):
        return slot < far_slot

    def goes_down(slot):
        return slot == 0 or far_slot < slot < 2 * far_slot

    def plane(slot, way):
        return copy(
            row_id, slot, None, (to_x, to_y)[way], p_send.at[slot, way], p_recv.at[slot, way], slot == 0
        )

    def relay(slot, way):
        row = (x_row, y_row)[way]
        target = (to_y, to_x)[way]
        return copy(row, slot, way, target, d_send.at[slot, way], d_recv.at[slot, way])

    def across(slot, kind):
        row = (row_id, x_row, y_row, diag_row, diag_row)[kind]
        piece = (None, None, None, 0, 1)[kind]
        return copy(
            row, slot, piece, to_core, c_send.at[slot, kind], c_recv.at[slot, kind],
            slot == 0 and kind == 0,
        )

    def stage_own(slot):
        def act():
            if slot:
                copy(row_id, slot, None, up, z_send.at[slot, 0], z_recv.at[slot]).wait_recv()
            if goes_up(slot):
                pl.when(has_up)(lambda: z_up(slot).start())
            if goes_down(slot):
                pl.when(has_down)(lambda: z_down(slot).start())
            plane(slot, 0).start()
            plane(slot, 1).start()
            across(slot, 0).start()

        valid(slot, act)

    def stage_relay(slot):
        def act():
            for way in range(2):
                plane_in = (x_row, y_row)[way]
                copy(
                    plane_in, slot, None, to_x, p_send.at[slot, way], p_recv.at[slot, way]
                ).wait_recv()
                relay(slot, way).start()
                across(slot, 1 + way).start()

        valid(slot, act)

    def stage_diag(slot):
        def act():
            for way in range(2):
                copy(
                    diag_row, slot, way, to_x, d_send.at[slot, way], d_recv.at[slot, way]
                ).wait_recv()
                across(slot, 3 + way).start()

        valid(slot, act)

    def stage_end(slot):
        def act():
            if goes_up(slot):
                pl.when(has_up)(lambda: z_up(slot).wait_send())
            if goes_down(slot):
                pl.when(has_down)(lambda: z_down(slot).wait_send())
            for way in range(2):
                plane(slot, way).wait_send()
                relay(slot, way).wait_send()
            for kind in range(5):
                across(slot, kind).wait()

        valid(slot, act)

    keep_own = pltpu.make_async_copy(own_ref, part(row_id, 0, None), local_sem)
    keep_own.start()
    for turn in range(len(slots) + 2):
        if turn < len(slots):
            stage_own(slots[turn])
        if 1 <= turn <= len(slots):
            stage_relay(slots[turn - 1])
        if turn >= 2:
            stage_diag(slots[turn - 2])
    for slot in slots:
        stage_end(slot)
    keep_own.wait()


def gather_blocks(own):
    rows, cols = own.shape
    columns = lax.axis_size("col")
    count = lax.axis_size("row") * columns
    slots = columns - 1
    dma = pltpu.SemaphoreType.DMA
    anywhere = pl.BlockSpec(memory_space=pl.ANY)
    return pl.pallas_call(
        gather_kernel,
        out_shape=jax.ShapeDtypeStruct((count, rows, cols), own.dtype),
        in_specs=[anywhere],
        out_specs=anywhere,
        scratch_shapes=[
            dma((slots, 2)), dma((slots,)),
            dma((slots, 2)), dma((slots, 2)),
            dma((slots, 2)), dma((slots, 2)),
            dma((slots, 5)), dma((slots, 5)),
            dma,
        ],
        compiler_params=pltpu.CompilerParams(collective_id=0, has_side_effects=True),
    )(own)


def per_device_gather(upper_stored, block_cells):
    rows, cols = upper_stored.shape
    order_total = rows * lax.axis_size("row")
    columns = order_total // cols
    blocks = gather_blocks(masked_density(upper_stored, block_cells))
    lanes = jnp.zeros((8, order_total), jnp.int32).at[:3].set(jnp.repeat(block_cells, BLK, axis=0).T)
    vmem = pl.BlockSpec(memory_space=pltpu.VMEM)
    return pl.pallas_call(
        purify_kernel,
        out_shape=jax.ShapeDtypeStruct((rows, cols), jnp.bfloat16),
        in_specs=[
            pl.BlockSpec(memory_space=pltpu.SMEM),
            vmem,
            pl.BlockSpec(memory_space=pl.ANY),
        ],
        out_specs=vmem,
        scratch_shapes=[
            pltpu.VMEM((order_total, order_total), jnp.bfloat16),
            pltpu.VMEM((rows, order_total), jnp.bfloat16),
            pltpu.VMEM((rows, cols), jnp.float32),
            pltpu.SemaphoreType.DMA((columns * columns,)),
        ],
        compiler_params=pltpu.CompilerParams(vmem_limit_bytes=48 * 2**20),
    )(block_cells, lanes, blocks)


def per_device(upper_stored, block_cells):
    order_total = upper_stored.shape[0] * lax.axis_size("row")
    if lax.axis_size("row") != 4 or order_total * order_total * 2 > 24 * 2**20:
        return per_device_ring(upper_stored, block_cells)
    return per_device_gather(upper_stored, block_cells)


def solution(mesh):
    return jax.shard_map(
        per_device,
        mesh=mesh,
        in_specs=(P("row", "col"), P()),
        out_specs=P("row", "col"),
        check_vma=False,
    )
```

```python
import math

import jax
import jax.numpy as jnp
from jax import lax
from jax.experimental import pallas as pl
from jax.experimental.pallas import tpu as pltpu
from jax.sharding import PartitionSpec as P

BLK = 64
BOX = 16
NEAR = 40
FAR = 90


def shifted_2(array, axis, by):
    length = lax.axis_size(axis)
    return lax.ppermute(array, axis, [(i, (i + by) % length) for i in range(length)])


def partner(value, axis, bit):
    mask = 2**bit
    pairs = [(source, source ^ mask) for source in range(lax.axis_size(axis))]
    return lax.ppermute(value, axis, pairs)


def cell_mask(block_cells, row_start, row_count, col_start, col_count, bound_sq):
    row_cells = lax.dynamic_slice_in_dim(block_cells, row_start, row_count, 0)
    col_cells = lax.dynamic_slice_in_dim(block_cells, col_start, col_count, 0)
    offset_abs = jnp.abs(row_cells[:, None, :] - col_cells[None, :, :])
    wrapped = jnp.minimum(offset_abs, BOX - offset_abs)
    return jnp.sum(wrapped * wrapped, axis=2) <= bound_sq


def block_keep(matrix_tile, keep_mask):
    row_count, col_count = matrix_tile.shape
    row_blocks, col_blocks = keep_mask.shape
    shaped = matrix_tile.reshape(
        row_blocks, row_count // row_blocks, col_blocks, col_count // col_blocks
    )
    kept = jnp.where(keep_mask[:, None, :, None], shaped, jnp.zeros_like(shaped))
    return kept.reshape(row_count, col_count)


def own_part(matrix_tile, layer_bit, half_width):
    return jnp.where(layer_bit == 0, matrix_tile[:, :half_width], matrix_tile[:, half_width:])


def partner_part(matrix_tile, layer_bit, half_width):
    return jnp.where(layer_bit == 0, matrix_tile[:, half_width:], matrix_tile[:, :half_width])


def join_halves(own_piece, partner_piece, layer_bit):
    first_order = jnp.concatenate([own_piece, partner_piece], 1)
    second_order = jnp.concatenate([partner_piece, own_piece], 1)
    return jnp.where(layer_bit == 0, first_order, second_order)


def skew_left(operand, row_id, layer_bit, grid_size):
    steps_wanted = (row_id + layer_bit * (grid_size // 2)) % grid_size
    for bit_pos in range((grid_size - 1).bit_length()):
        shifted = shifted_2(operand, "col", -(2 << bit_pos))
        operand = jnp.where((steps_wanted >> bit_pos) % 2 == 1, shifted, operand)
    return operand


def skew_right(operand, tile_col, layer_bit, grid_size):
    steps_wanted = (tile_col + layer_bit * (grid_size // 2)) % grid_size
    for bit_pos in range((grid_size - 1).bit_length()):
        shifted = shifted_2(operand, "row", -(1 << bit_pos))
        operand = jnp.where((steps_wanted >> bit_pos) % 2 == 1, shifted, operand)
    return operand


def cannon_half(left, right, grid_size):
    running = jnp.zeros((left.shape[0], right.shape[1]), jnp.float32)
    for section in range(grid_size // 2):
        running = running + jnp.dot(left, right, preferred_element_type=jnp.float32)
        if section + 1 < grid_size // 2:
            left = shifted_2(left, "col", -2)
            right = shifted_2(right, "row", -1)
    return running


def per_device_ring(upper_stored, block_cells):
    grid_size = lax.axis_size("row")
    row_id = lax.axis_index("row")
    col_id = lax.axis_index("col")
    layer_bit = col_id % 2
    tile_col = col_id // 2
    tile_side, half_width = upper_stored.shape
    order_total = tile_side * grid_size
    tile_blocks = tile_side // BLK
    half_blocks = half_width // BLK
    slab_width = half_width // grid_size
    stacked = lax.all_to_all(
        lax.all_to_all(upper_stored, "row", split_axis=1, concat_axis=0, tiled=True),
        "col",
        split_axis=0,
        concat_axis=1,
        tiled=True,
    )
    gathered = lax.all_to_all(stacked.T, "row", split_axis=0, concat_axis=0, tiled=True)
    mirrored = (
        gathered.reshape(grid_size, 2, slab_width, half_width)
        .transpose(1, 0, 2, 3)
        .reshape(tile_side, half_width)
    )
    global_rows = row_id * tile_side + lax.broadcasted_iota(jnp.int32, (tile_side, half_width), 0)
    global_cols = col_id * half_width + lax.broadcasted_iota(jnp.int32, (tile_side, half_width), 1)
    symmetric = jnp.where(global_rows <= global_cols, upper_stored, mirrored)
    near_own = cell_mask(
        block_cells, row_id * tile_blocks, tile_blocks, col_id * half_blocks, half_blocks, NEAR
    )
    diagonal = jnp.where(global_rows == global_cols, 0.5, 0.0).astype(jnp.float32)
    value_scale = 2.0 / math.sqrt(order_total)
    own_density = block_keep(
        diagonal + value_scale * symmetric.astype(jnp.float32), near_own
    ).astype(jnp.bfloat16)
    partner_density = partner(own_density, "col", 0)
    density = join_halves(own_density, partner_density, layer_bit)
    right_start = skew_right(density, tile_col, layer_bit, grid_size)
    left_start = skew_left(density, row_id, layer_bit, grid_size)
    running = cannon_half(left_start, right_start, grid_size)
    far_full = cell_mask(
        block_cells, row_id * tile_blocks, tile_blocks, tile_col * tile_blocks, tile_blocks, FAR
    )
    partner_running = partner(running, "col", 0)
    square = block_keep(running + partner_running, far_full)
    square_low = square.astype(jnp.bfloat16)
    own_square = own_part(square, layer_bit, half_width)
    right_again = skew_right(density, tile_col, layer_bit, grid_size)
    left_again = skew_left(square_low, row_id, layer_bit, grid_size)
    cubic_running = cannon_half(left_again, right_again, grid_size)
    received_cubic = partner(partner_part(cubic_running, layer_bit, half_width), "col", 0)
    cubic = own_part(cubic_running, layer_bit, half_width) + received_cubic
    return block_keep(3.0 * own_square - 2.0 * cubic, near_own).astype(jnp.bfloat16)


def wrapped_square(row_cells, col_cells):
    total = 0
    for axis in range(3):
        offset = jnp.abs(row_cells[axis] - col_cells[axis])
        wrapped = jnp.minimum(offset, BOX - offset)
        total = total + wrapped * wrapped
    return total


def masked_density(upper_stored, block_cells):
    rows, cols = upper_stored.shape
    row_start = lax.axis_index("row") * rows
    col_start = lax.axis_index("col") * cols
    order_total = rows * lax.axis_size("row")
    row_cells = lax.dynamic_slice_in_dim(block_cells, row_start // BLK, rows // BLK, 0)
    col_cells = lax.dynamic_slice_in_dim(block_cells, col_start // BLK, cols // BLK, 0)
    row_cells = jnp.repeat(row_cells, BLK, axis=0)
    col_cells = jnp.repeat(col_cells, BLK, axis=0)
    near = wrapped_square(
        [row_cells[:, a][:, None] for a in range(3)], [col_cells[:, a][None, :] for a in range(3)]
    )
    global_rows = row_start + lax.broadcasted_iota(jnp.int32, (rows, cols), 0)
    global_cols = col_start + lax.broadcasted_iota(jnp.int32, (rows, cols), 1)
    diagonal = jnp.where(global_rows == global_cols, 0.5, 0.0).astype(jnp.float32)
    value = diagonal + (2.0 / math.sqrt(order_total)) * upper_stored.astype(jnp.float32)
    return jnp.where(near <= NEAR, value, 0.0).astype(jnp.bfloat16)


def purify_kernel(cells_ref, lanes_ref, blocks_ref, out_ref, density, square_low, own, sems):
    rows, cols = out_ref.shape
    order_total = density.shape[0]
    columns = order_total // cols
    per_row = rows // cols
    row_id = lax.axis_index("row")
    col_id = lax.axis_index("col")

    def load(i, j):
        return pltpu.make_async_copy(
            blocks_ref.at[(i // per_row) * columns + j, pl.ds((i % per_row) * cols, cols)],
            density.at[pl.ds(i * cols, cols), pl.ds(j * cols, cols)],
            sems.at[i * columns + j],
        )

    pairs = [(i, j) for j in range(columns) for i in range(j + 1)]
    for i, j in pairs:
        load(i, j).start()
    below = lax.broadcasted_iota(jnp.int32, (cols, cols), 0) > lax.broadcasted_iota(
        jnp.int32, (cols, cols), 1
    )
    for i, j in pairs:
        load(i, j).wait()
        upper = density[i * cols : (i + 1) * cols, j * cols : (j + 1) * cols]
        flipped = upper.T
        if i == j:
            flipped = jnp.where(below, flipped, upper)
        density[j * cols : (j + 1) * cols, i * cols : (i + 1) * cols] = flipped

    def keep(value, lanes, bound):
        pieces = []
        for block in range(rows // BLK):
            row = row_id * (rows // BLK) + block
            distance = wrapped_square(
                [cells_ref[row, a] for a in range(3)], [lanes[a : a + 1, :] for a in range(3)]
            )
            piece = value[block * BLK : (block + 1) * BLK]
            pieces.append(jnp.where(distance <= bound, piece, 0.0))
        return jnp.concatenate(pieces, 0)

    own_rows = pl.ds(pl.multiple_of(row_id * rows, rows), rows)

    @pl.loop(0, columns)
    def _(j):
        here = pl.ds(pl.multiple_of(j * cols, cols), cols)
        product = jnp.dot(
            density[own_rows, :], density[:, here], preferred_element_type=jnp.float32
        )
        square = keep(product, lanes_ref[:, here], FAR)
        square_low[:, here] = square.astype(jnp.bfloat16)

        @pl.when(j == col_id)
        def _():
            own[...] = square

    mine = pl.ds(pl.multiple_of(col_id * cols, cols), cols)
    cubic = jnp.dot(square_low[...], density[:, mine], preferred_element_type=jnp.float32)
    result = 3.0 * own[...] - 2.0 * cubic
    out_ref[...] = keep(result, lanes_ref[:, mine], NEAR).astype(jnp.bfloat16)


def gather_kernel(
    own_ref, blocks_ref, z_send, z_recv, p_send, p_recv, d_send, d_recv, c_send, c_recv, local_sem
):
    rows = own_ref.shape[0]
    half = rows // 2
    columns = lax.axis_size("col")
    layers = columns // 2
    row_id = lax.axis_index("row")
    col_id = lax.axis_index("col")
    z, core = col_id // 2, col_id % 2
    x_row = row_id + 1 - 2 * (row_id % 2)
    y_row = (row_id + 2) % 4
    diag_row = (x_row + 2) % 4
    mesh_id = pl.DeviceIdType.MESH
    to_x, to_y = (x_row, col_id), (y_row, col_id)
    to_core = (row_id, col_id + 1 - 2 * core)
    up, down = (row_id, col_id + 2), (row_id, col_id - 2)
    has_up, has_down = z + 1 < layers, z > 0

    barrier = pltpu.get_barrier_semaphore()
    for target in (to_x, to_y, to_core):
        pl.semaphore_signal(barrier, inc=1, device_id=target, device_id_type=mesh_id)

    @pl.when(has_up)
    def _():
        pl.semaphore_signal(barrier, inc=1, device_id=up, device_id_type=mesh_id)

    @pl.when(has_down)
    def _():
        pl.semaphore_signal(barrier, inc=1, device_id=down, device_id_type=mesh_id)

    pl.semaphore_wait(barrier, 3 + has_up.astype(jnp.int32) + has_down.astype(jnp.int32))

    far_slot = layers - 1
    slots = [0]
    for step in range(far_slot):
        slots += [1 + step, 1 + far_slot + step]

    def layer(slot):
        if slot == 0:
            return z
        if slot <= far_slot:
            return z - slot
        return z + slot - far_slot

    def valid(slot, act):
        if slot == 0:
            act()
        elif slot <= far_slot:
            pl.when(z >= slot)(act)
        else:
            pl.when(z + slot - far_slot < layers)(act)

    def used(row, slot, act):
        pl.when(row * rows < (2 * layer(slot) + 2) * own_ref.shape[1])(act)

    def part(row, slot, piece):
        index = row * columns + 2 * layer(slot) + core
        block = blocks_ref.at[index]
        return block if piece is None else block.at[pl.ds(piece * half, half)]

    def copy(row, slot, piece, target, send, recv, first=False):
        place = part(row, slot, piece)
        return pltpu.make_async_remote_copy(
            src_ref=own_ref if first else place,
            dst_ref=place,
            send_sem=send,
            recv_sem=recv,
            device_id=target,
            device_id_type=mesh_id,
        )

    def z_up(slot):
        return copy(row_id, slot, None, up, z_send.at[slot, 0], z_recv.at[slot + 1], slot == 0)

    def z_down(slot):
        later = 1 + far_slot if slot == 0 else slot + 1
        return copy(row_id, slot, None, down, z_send.at[slot, 1], z_recv.at[later], slot == 0)

    def goes_up(slot):
        return slot < far_slot

    def goes_down(slot):
        return slot == 0 or far_slot < slot < 2 * far_slot

    def plane(slot, way):
        return copy(
            row_id, slot, None, (to_x, to_y)[way], p_send.at[slot, way], p_recv.at[slot, way], slot == 0
        )

    def relay(slot, way):
        row = (x_row, y_row)[way]
        target = (to_y, to_x)[way]
        return copy(row, slot, way, target, d_send.at[slot, way], d_recv.at[slot, way])

    def across(slot, kind):
        row = (row_id, x_row, y_row, diag_row, diag_row)[kind]
        piece = (None, None, None, 0, 1)[kind]
        return copy(
            row, slot, piece, to_core, c_send.at[slot, kind], c_recv.at[slot, kind],
            slot == 0 and kind == 0,
        )

    def stage_own(slot):
        def act():
            if slot:
                copy(row_id, slot, None, up, z_send.at[slot, 0], z_recv.at[slot]).wait_recv()
            if goes_up(slot):
                pl.when(has_up)(lambda: z_up(slot).start())
            if goes_down(slot):
                pl.when(has_down)(lambda: z_down(slot).start())
            plane(slot, 0).start()
            plane(slot, 1).start()
            across(slot, 0).start()

        valid(slot, lambda: used(row_id, slot, act))

    def stage_relay(slot):
        def one(way):
            plane_in = (x_row, y_row)[way]
            copy(
                plane_in, slot, None, to_x, p_send.at[slot, way], p_recv.at[slot, way]
            ).wait_recv()
            relay(slot, way).start()
            across(slot, 1 + way).start()

        def act():
            used(x_row, slot, lambda: one(0))
            used(y_row, slot, lambda: one(1))

        valid(slot, act)

    def stage_diag(slot):
        def act():
            for way in range(2):
                copy(
                    diag_row, slot, way, to_x, d_send.at[slot, way], d_recv.at[slot, way]
                ).wait_recv()
                across(slot, 3 + way).start()

        valid(slot, lambda: used(diag_row, slot, act))

    def stage_end(slot):
        def own_end():
            if goes_up(slot):
                pl.when(has_up)(lambda: z_up(slot).wait_send())
            if goes_down(slot):
                pl.when(has_down)(lambda: z_down(slot).wait_send())
            for way in range(2):
                plane(slot, way).wait_send()
            across(slot, 0).wait()

        def relay_end(way):
            relay(slot, way).wait_send()
            across(slot, 1 + way).wait()

        def diag_end():
            across(slot, 3).wait()
            across(slot, 4).wait()

        def act():
            used(row_id, slot, own_end)
            used(x_row, slot, lambda: relay_end(0))
            used(y_row, slot, lambda: relay_end(1))
            used(diag_row, slot, diag_end)

        valid(slot, act)

    keep_own = pltpu.make_async_copy(own_ref, part(row_id, 0, None), local_sem)
    keep_own.start()
    for turn in range(len(slots) + 2):
        if turn < len(slots):
            stage_own(slots[turn])
        if 1 <= turn <= len(slots):
            stage_relay(slots[turn - 1])
        if turn >= 2:
            stage_diag(slots[turn - 2])
    for slot in slots:
        stage_end(slot)
    keep_own.wait()


def gather_blocks(own):
    rows, cols = own.shape
    columns = lax.axis_size("col")
    count = lax.axis_size("row") * columns
    slots = columns - 1
    dma = pltpu.SemaphoreType.DMA
    anywhere = pl.BlockSpec(memory_space=pl.ANY)
    return pl.pallas_call(
        gather_kernel,
        out_shape=jax.ShapeDtypeStruct((count, rows, cols), own.dtype),
        in_specs=[anywhere],
        out_specs=anywhere,
        scratch_shapes=[
            dma((slots, 2)), dma((slots,)),
            dma((slots, 2)), dma((slots, 2)),
            dma((slots, 2)), dma((slots, 2)),
            dma((slots, 5)), dma((slots, 5)),
            dma,
        ],
        compiler_params=pltpu.CompilerParams(collective_id=0, has_side_effects=True),
    )(own)


def per_device_gather(upper_stored, block_cells):
    rows, cols = upper_stored.shape
    order_total = rows * lax.axis_size("row")
    columns = order_total // cols
    blocks = gather_blocks(masked_density(upper_stored, block_cells))
    lanes = jnp.zeros((8, order_total), jnp.int32).at[:3].set(jnp.repeat(block_cells, BLK, axis=0).T)
    vmem = pl.BlockSpec(memory_space=pltpu.VMEM)
    return pl.pallas_call(
        purify_kernel,
        out_shape=jax.ShapeDtypeStruct((rows, cols), jnp.bfloat16),
        in_specs=[
            pl.BlockSpec(memory_space=pltpu.SMEM),
            vmem,
            pl.BlockSpec(memory_space=pl.ANY),
        ],
        out_specs=vmem,
        scratch_shapes=[
            pltpu.VMEM((order_total, order_total), jnp.bfloat16),
            pltpu.VMEM((rows, order_total), jnp.bfloat16),
            pltpu.VMEM((rows, cols), jnp.float32),
            pltpu.SemaphoreType.DMA((columns * columns,)),
        ],
        compiler_params=pltpu.CompilerParams(vmem_limit_bytes=48 * 2**20),
    )(block_cells, lanes, blocks)


def per_device(upper_stored, block_cells):
    order_total = upper_stored.shape[0] * lax.axis_size("row")
    if lax.axis_size("row") != 4 or order_total * order_total * 2 > 24 * 2**20:
        return per_device_ring(upper_stored, block_cells)
    return per_device_gather(upper_stored, block_cells)


def solution(mesh):
    return jax.shard_map(
        per_device,
        mesh=mesh,
        in_specs=(P("row", "col"), P()),
        out_specs=P("row", "col"),
        check_vma=False,
    )
```

```python
import math

import jax
import jax.numpy as jnp
from jax import lax
from jax.experimental import pallas as pl
from jax.experimental.pallas import tpu as pltpu
from jax.sharding import PartitionSpec as P

BLK = 64
BOX = 16
NEAR = 40
FAR = 90


def shifted_2(array, axis, by):
    length = lax.axis_size(axis)
    return lax.ppermute(array, axis, [(i, (i + by) % length) for i in range(length)])


def partner(value, axis, bit):
    mask = 2**bit
    pairs = [(source, source ^ mask) for source in range(lax.axis_size(axis))]
    return lax.ppermute(value, axis, pairs)


def cell_mask(block_cells, row_start, row_count, col_start, col_count, bound_sq):
    row_cells = lax.dynamic_slice_in_dim(block_cells, row_start, row_count, 0)
    col_cells = lax.dynamic_slice_in_dim(block_cells, col_start, col_count, 0)
    offset_abs = jnp.abs(row_cells[:, None, :] - col_cells[None, :, :])
    wrapped = jnp.minimum(offset_abs, BOX - offset_abs)
    return jnp.sum(wrapped * wrapped, axis=2) <= bound_sq


def block_keep(matrix_tile, keep_mask):
    row_count, col_count = matrix_tile.shape
    row_blocks, col_blocks = keep_mask.shape
    shaped = matrix_tile.reshape(
        row_blocks, row_count // row_blocks, col_blocks, col_count // col_blocks
    )
    kept = jnp.where(keep_mask[:, None, :, None], shaped, jnp.zeros_like(shaped))
    return kept.reshape(row_count, col_count)


def own_part(matrix_tile, layer_bit, half_width):
    return jnp.where(layer_bit == 0, matrix_tile[:, :half_width], matrix_tile[:, half_width:])


def partner_part(matrix_tile, layer_bit, half_width):
    return jnp.where(layer_bit == 0, matrix_tile[:, half_width:], matrix_tile[:, :half_width])


def join_halves(own_piece, partner_piece, layer_bit):
    first_order = jnp.concatenate([own_piece, partner_piece], 1)
    second_order = jnp.concatenate([partner_piece, own_piece], 1)
    return jnp.where(layer_bit == 0, first_order, second_order)


def skew_left(operand, row_id, layer_bit, grid_size):
    steps_wanted = (row_id + layer_bit * (grid_size // 2)) % grid_size
    for bit_pos in range((grid_size - 1).bit_length()):
        shifted = shifted_2(operand, "col", -(2 << bit_pos))
        operand = jnp.where((steps_wanted >> bit_pos) % 2 == 1, shifted, operand)
    return operand


def skew_right(operand, tile_col, layer_bit, grid_size):
    steps_wanted = (tile_col + layer_bit * (grid_size // 2)) % grid_size
    for bit_pos in range((grid_size - 1).bit_length()):
        shifted = shifted_2(operand, "row", -(1 << bit_pos))
        operand = jnp.where((steps_wanted >> bit_pos) % 2 == 1, shifted, operand)
    return operand


def cannon_half(left, right, grid_size):
    running = jnp.zeros((left.shape[0], right.shape[1]), jnp.float32)
    for section in range(grid_size // 2):
        running = running + jnp.dot(left, right, preferred_element_type=jnp.float32)
        if section + 1 < grid_size // 2:
            left = shifted_2(left, "col", -2)
            right = shifted_2(right, "row", -1)
    return running


def per_device_ring(upper_stored, block_cells):
    grid_size = lax.axis_size("row")
    row_id = lax.axis_index("row")
    col_id = lax.axis_index("col")
    layer_bit = col_id % 2
    tile_col = col_id // 2
    tile_side, half_width = upper_stored.shape
    order_total = tile_side * grid_size
    tile_blocks = tile_side // BLK
    half_blocks = half_width // BLK
    slab_width = half_width // grid_size
    stacked = lax.all_to_all(
        lax.all_to_all(upper_stored, "row", split_axis=1, concat_axis=0, tiled=True),
        "col",
        split_axis=0,
        concat_axis=1,
        tiled=True,
    )
    gathered = lax.all_to_all(stacked.T, "row", split_axis=0, concat_axis=0, tiled=True)
    mirrored = (
        gathered.reshape(grid_size, 2, slab_width, half_width)
        .transpose(1, 0, 2, 3)
        .reshape(tile_side, half_width)
    )
    global_rows = row_id * tile_side + lax.broadcasted_iota(jnp.int32, (tile_side, half_width), 0)
    global_cols = col_id * half_width + lax.broadcasted_iota(jnp.int32, (tile_side, half_width), 1)
    symmetric = jnp.where(global_rows <= global_cols, upper_stored, mirrored)
    near_own = cell_mask(
        block_cells, row_id * tile_blocks, tile_blocks, col_id * half_blocks, half_blocks, NEAR
    )
    diagonal = jnp.where(global_rows == global_cols, 0.5, 0.0).astype(jnp.float32)
    value_scale = 2.0 / math.sqrt(order_total)
    own_density = block_keep(
        diagonal + value_scale * symmetric.astype(jnp.float32), near_own
    ).astype(jnp.bfloat16)
    partner_density = partner(own_density, "col", 0)
    density = join_halves(own_density, partner_density, layer_bit)
    right_start = skew_right(density, tile_col, layer_bit, grid_size)
    left_start = skew_left(density, row_id, layer_bit, grid_size)
    running = cannon_half(left_start, right_start, grid_size)
    far_full = cell_mask(
        block_cells, row_id * tile_blocks, tile_blocks, tile_col * tile_blocks, tile_blocks, FAR
    )
    partner_running = partner(running, "col", 0)
    square = block_keep(running + partner_running, far_full)
    square_low = square.astype(jnp.bfloat16)
    own_square = own_part(square, layer_bit, half_width)
    right_again = skew_right(density, tile_col, layer_bit, grid_size)
    left_again = skew_left(square_low, row_id, layer_bit, grid_size)
    cubic_running = cannon_half(left_again, right_again, grid_size)
    received_cubic = partner(partner_part(cubic_running, layer_bit, half_width), "col", 0)
    cubic = own_part(cubic_running, layer_bit, half_width) + received_cubic
    return block_keep(3.0 * own_square - 2.0 * cubic, near_own).astype(jnp.bfloat16)


def wrapped_square(row_cells, col_cells):
    total = 0
    for axis in range(3):
        offset = jnp.abs(row_cells[axis] - col_cells[axis])
        wrapped = jnp.minimum(offset, BOX - offset)
        total = total + wrapped * wrapped
    return total


def masked_density(upper_stored, block_cells):
    rows, cols = upper_stored.shape
    row_start = lax.axis_index("row") * rows
    col_start = lax.axis_index("col") * cols
    order_total = rows * lax.axis_size("row")
    row_cells = lax.dynamic_slice_in_dim(block_cells, row_start // BLK, rows // BLK, 0)
    col_cells = lax.dynamic_slice_in_dim(block_cells, col_start // BLK, cols // BLK, 0)
    row_cells = jnp.repeat(row_cells, BLK, axis=0)
    col_cells = jnp.repeat(col_cells, BLK, axis=0)
    near = wrapped_square(
        [row_cells[:, a][:, None] for a in range(3)], [col_cells[:, a][None, :] for a in range(3)]
    )
    global_rows = row_start + lax.broadcasted_iota(jnp.int32, (rows, cols), 0)
    global_cols = col_start + lax.broadcasted_iota(jnp.int32, (rows, cols), 1)
    diagonal = jnp.where(global_rows == global_cols, 0.5, 0.0).astype(jnp.float32)
    value = diagonal + (2.0 / math.sqrt(order_total)) * upper_stored.astype(jnp.float32)
    return jnp.where(near <= NEAR, value, 0.0).astype(jnp.bfloat16)


def purify_kernel(cells_ref, lanes_ref, blocks_ref, out_ref, density, square_low, own, sems):
    rows, cols = out_ref.shape
    order_total = density.shape[0]
    columns = order_total // cols
    per_row = rows // cols
    row_id = lax.axis_index("row")
    col_id = lax.axis_index("col")

    def load(i, j):
        return pltpu.make_async_copy(
            blocks_ref.at[(i // per_row) * columns + j, pl.ds((i % per_row) * cols, cols)],
            density.at[pl.ds(i * cols, cols), pl.ds(j * cols, cols)],
            sems.at[i * columns + j],
        )

    pairs = [(i, j) for j in range(columns) for i in range(j + 1)]
    for i, j in pairs:
        load(i, j).start()
    below = lax.broadcasted_iota(jnp.int32, (cols, cols), 0) > lax.broadcasted_iota(
        jnp.int32, (cols, cols), 1
    )
    for i, j in pairs:
        load(i, j).wait()
        upper = density[i * cols : (i + 1) * cols, j * cols : (j + 1) * cols]
        flipped = upper.T
        if i == j:
            flipped = jnp.where(below, flipped, upper)
        density[j * cols : (j + 1) * cols, i * cols : (i + 1) * cols] = flipped

    def keep(value, lanes, bound):
        pieces = []
        for block in range(rows // BLK):
            row = row_id * (rows // BLK) + block
            distance = wrapped_square(
                [cells_ref[row, a] for a in range(3)], [lanes[a : a + 1, :] for a in range(3)]
            )
            piece = value[block * BLK : (block + 1) * BLK]
            pieces.append(jnp.where(distance <= bound, piece, 0.0))
        return jnp.concatenate(pieces, 0)

    own_rows = pl.ds(pl.multiple_of(row_id * rows, rows), rows)

    @pl.loop(0, columns)
    def _(j):
        here = pl.ds(pl.multiple_of(j * cols, cols), cols)
        product = jnp.dot(
            density[own_rows, :], density[:, here], preferred_element_type=jnp.float32
        )
        square = keep(product, lanes_ref[:, here], FAR)
        square_low[:, here] = square.astype(jnp.bfloat16)

        @pl.when(j == col_id)
        def _():
            own[...] = square

    mine = pl.ds(pl.multiple_of(col_id * cols, cols), cols)
    cubic = jnp.dot(square_low[...], density[:, mine], preferred_element_type=jnp.float32)
    result = 3.0 * own[...] - 2.0 * cubic
    out_ref[...] = keep(result, lanes_ref[:, mine], NEAR).astype(jnp.bfloat16)


def gather_kernel(
    own_ref, blocks_ref, z_send, z_recv, p_send, p_recv, d_send, d_recv, c_send, c_recv, local_sem
):
    rows = own_ref.shape[0]
    cut = rows * 3 // 8 // 16 * 16
    columns = lax.axis_size("col")
    layers = columns // 2
    row_id = lax.axis_index("row")
    col_id = lax.axis_index("col")
    z, core = col_id // 2, col_id % 2
    x_row = row_id + 1 - 2 * (row_id % 2)
    y_row = (row_id + 2) % 4
    diag_row = (x_row + 2) % 4
    mesh_id = pl.DeviceIdType.MESH
    to_x, to_y = (x_row, col_id), (y_row, col_id)
    to_core = (row_id, col_id + 1 - 2 * core)
    up, down = (row_id, col_id + 2), (row_id, col_id - 2)
    has_up, has_down = z + 1 < layers, z > 0

    barrier = pltpu.get_barrier_semaphore()
    for target in (to_x, to_y, to_core):
        pl.semaphore_signal(barrier, inc=1, device_id=target, device_id_type=mesh_id)

    @pl.when(has_up)
    def _():
        pl.semaphore_signal(barrier, inc=1, device_id=up, device_id_type=mesh_id)

    @pl.when(has_down)
    def _():
        pl.semaphore_signal(barrier, inc=1, device_id=down, device_id_type=mesh_id)

    pl.semaphore_wait(barrier, 3 + has_up.astype(jnp.int32) + has_down.astype(jnp.int32))

    far_slot = layers - 1
    slots = [0]
    for step in range(far_slot):
        slots += [1 + step, 1 + far_slot + step]

    def layer(slot):
        if slot == 0:
            return z
        if slot <= far_slot:
            return z - slot
        return z + slot - far_slot

    def valid(slot, act):
        if slot == 0:
            act()
        elif slot <= far_slot:
            pl.when(z >= slot)(act)
        else:
            pl.when(z + slot - far_slot < layers)(act)

    def used(row, slot, act):
        pl.when(row * rows < (2 * layer(slot) + 2) * own_ref.shape[1])(act)

    def part(row, slot, piece):
        index = row * columns + 2 * layer(slot) + core
        block = blocks_ref.at[index]
        if piece is None:
            return block
        return block.at[pl.ds(0, cut) if piece == 0 else pl.ds(cut, rows - cut)]

    def copy(row, slot, piece, target, send, recv, first=False):
        place = part(row, slot, piece)
        return pltpu.make_async_remote_copy(
            src_ref=own_ref if first else place,
            dst_ref=place,
            send_sem=send,
            recv_sem=recv,
            device_id=target,
            device_id_type=mesh_id,
        )

    def z_up(slot):
        return copy(row_id, slot, None, up, z_send.at[slot, 0], z_recv.at[slot + 1], slot == 0)

    def z_down(slot):
        later = 1 + far_slot if slot == 0 else slot + 1
        return copy(row_id, slot, None, down, z_send.at[slot, 1], z_recv.at[later], slot == 0)

    def goes_up(slot):
        return slot < far_slot

    def goes_down(slot):
        return slot == 0 or far_slot < slot < 2 * far_slot

    def plane(slot, way):
        return copy(
            row_id, slot, None, (to_x, to_y)[way], p_send.at[slot, way], p_recv.at[slot, way], slot == 0
        )

    def relay(slot, way, piece):
        row = (x_row, y_row)[way]
        target = (to_y, to_x)[way]
        return copy(
            row, slot, piece, target, d_send.at[slot, 2 * way + piece], d_recv.at[slot, piece]
        )

    def each_relay(slot, way, act):
        row = (x_row, y_row)[way]
        first = (row != 1, row == 2) if way == 0 else (row == 1, row != 2)
        for piece in range(2):
            pl.when(first[piece])(lambda piece=piece: act(relay(slot, way, piece)))

    def across(slot, kind):
        row = (row_id, x_row, y_row, diag_row, diag_row)[kind]
        piece = (None, None, None, 0, 1)[kind]
        return copy(
            row, slot, piece, to_core, c_send.at[slot, kind], c_recv.at[slot, kind],
            slot == 0 and kind == 0,
        )

    def stage_own(slot):
        def act():
            if slot:
                copy(row_id, slot, None, up, z_send.at[slot, 0], z_recv.at[slot]).wait_recv()
            if goes_up(slot):
                pl.when(has_up)(lambda: z_up(slot).start())
            if goes_down(slot):
                pl.when(has_down)(lambda: z_down(slot).start())
            plane(slot, 0).start()
            plane(slot, 1).start()
            across(slot, 0).start()

        valid(slot, lambda: used(row_id, slot, act))

    def stage_relay(slot):
        def one(way):
            plane_in = (x_row, y_row)[way]
            copy(
                plane_in, slot, None, to_x, p_send.at[slot, way], p_recv.at[slot, way]
            ).wait_recv()
            each_relay(slot, way, lambda c: c.start())
            across(slot, 1 + way).start()

        def act():
            used(x_row, slot, lambda: one(0))
            used(y_row, slot, lambda: one(1))

        valid(slot, act)

    def stage_diag(slot):
        def act():
            for way in range(2):
                copy(
                    diag_row, slot, way, to_x, d_send.at[slot, way], d_recv.at[slot, way]
                ).wait_recv()
                across(slot, 3 + way).start()

        valid(slot, lambda: used(diag_row, slot, act))

    def stage_end(slot):
        def own_end():
            if goes_up(slot):
                pl.when(has_up)(lambda: z_up(slot).wait_send())
            if goes_down(slot):
                pl.when(has_down)(lambda: z_down(slot).wait_send())
            for way in range(2):
                plane(slot, way).wait_send()
            across(slot, 0).wait()

        def relay_end(way):
            each_relay(slot, way, lambda c: c.wait_send())
            across(slot, 1 + way).wait()

        def diag_end():
            across(slot, 3).wait()
            across(slot, 4).wait()

        def act():
            used(row_id, slot, own_end)
            used(x_row, slot, lambda: relay_end(0))
            used(y_row, slot, lambda: relay_end(1))
            used(diag_row, slot, diag_end)

        valid(slot, act)

    keep_own = pltpu.make_async_copy(own_ref, part(row_id, 0, None), local_sem)
    keep_own.start()
    for turn in range(len(slots) + 2):
        if turn < len(slots):
            stage_own(slots[turn])
        if 1 <= turn <= len(slots):
            stage_relay(slots[turn - 1])
        if turn >= 2:
            stage_diag(slots[turn - 2])
    for slot in slots:
        stage_end(slot)
    keep_own.wait()


def gather_blocks(own):
    rows, cols = own.shape
    columns = lax.axis_size("col")
    count = lax.axis_size("row") * columns
    slots = columns - 1
    dma = pltpu.SemaphoreType.DMA
    anywhere = pl.BlockSpec(memory_space=pl.ANY)
    return pl.pallas_call(
        gather_kernel,
        out_shape=jax.ShapeDtypeStruct((count, rows, cols), own.dtype),
        in_specs=[anywhere],
        out_specs=anywhere,
        scratch_shapes=[
            dma((slots, 2)), dma((slots,)),
            dma((slots, 2)), dma((slots, 2)),
            dma((slots, 4)), dma((slots, 2)),
            dma((slots, 5)), dma((slots, 5)),
            dma,
        ],
        compiler_params=pltpu.CompilerParams(collective_id=0, has_side_effects=True),
    )(own)


def per_device_gather(upper_stored, block_cells):
    rows, cols = upper_stored.shape
    order_total = rows * lax.axis_size("row")
    columns = order_total // cols
    blocks = gather_blocks(masked_density(upper_stored, block_cells))
    lanes = jnp.zeros((8, order_total), jnp.int32).at[:3].set(jnp.repeat(block_cells, BLK, axis=0).T)
    vmem = pl.BlockSpec(memory_space=pltpu.VMEM)
    return pl.pallas_call(
        purify_kernel,
        out_shape=jax.ShapeDtypeStruct((rows, cols), jnp.bfloat16),
        in_specs=[
            pl.BlockSpec(memory_space=pltpu.SMEM),
            vmem,
            pl.BlockSpec(memory_space=pl.ANY),
        ],
        out_specs=vmem,
        scratch_shapes=[
            pltpu.VMEM((order_total, order_total), jnp.bfloat16),
            pltpu.VMEM((rows, order_total), jnp.bfloat16),
            pltpu.VMEM((rows, cols), jnp.float32),
            pltpu.SemaphoreType.DMA((columns * columns,)),
        ],
        compiler_params=pltpu.CompilerParams(vmem_limit_bytes=48 * 2**20),
    )(block_cells, lanes, blocks)


def per_device(upper_stored, block_cells):
    order_total = upper_stored.shape[0] * lax.axis_size("row")
    if lax.axis_size("row") != 4 or order_total * order_total * 2 > 24 * 2**20:
        return per_device_ring(upper_stored, block_cells)
    return per_device_gather(upper_stored, block_cells)


def solution(mesh):
    return jax.shard_map(
        per_device,
        mesh=mesh,
        in_specs=(P("row", "col"), P()),
        out_specs=P("row", "col"),
        check_vma=False,
    )
```

```python
import math

import jax
import jax.numpy as jnp
from jax import lax
from jax.experimental import pallas as pl
from jax.experimental.pallas import tpu as pltpu
from jax.sharding import PartitionSpec as P

BLK = 64
BOX = 16
NEAR = 40
FAR = 90


def shifted_2(array, axis, by):
    length = lax.axis_size(axis)
    return lax.ppermute(array, axis, [(i, (i + by) % length) for i in range(length)])


def partner(value, axis, bit):
    mask = 2**bit
    pairs = [(source, source ^ mask) for source in range(lax.axis_size(axis))]
    return lax.ppermute(value, axis, pairs)


def cell_mask(block_cells, row_start, row_count, col_start, col_count, bound_sq):
    row_cells = lax.dynamic_slice_in_dim(block_cells, row_start, row_count, 0)
    col_cells = lax.dynamic_slice_in_dim(block_cells, col_start, col_count, 0)
    offset_abs = jnp.abs(row_cells[:, None, :] - col_cells[None, :, :])
    wrapped = jnp.minimum(offset_abs, BOX - offset_abs)
    return jnp.sum(wrapped * wrapped, axis=2) <= bound_sq


def block_keep(matrix_tile, keep_mask):
    row_count, col_count = matrix_tile.shape
    row_blocks, col_blocks = keep_mask.shape
    shaped = matrix_tile.reshape(
        row_blocks, row_count // row_blocks, col_blocks, col_count // col_blocks
    )
    kept = jnp.where(keep_mask[:, None, :, None], shaped, jnp.zeros_like(shaped))
    return kept.reshape(row_count, col_count)


def own_part(matrix_tile, layer_bit, half_width):
    return jnp.where(layer_bit == 0, matrix_tile[:, :half_width], matrix_tile[:, half_width:])


def partner_part(matrix_tile, layer_bit, half_width):
    return jnp.where(layer_bit == 0, matrix_tile[:, half_width:], matrix_tile[:, :half_width])


def join_halves(own_piece, partner_piece, layer_bit):
    first_order = jnp.concatenate([own_piece, partner_piece], 1)
    second_order = jnp.concatenate([partner_piece, own_piece], 1)
    return jnp.where(layer_bit == 0, first_order, second_order)


def skew_left(operand, row_id, layer_bit, grid_size):
    steps_wanted = (row_id + layer_bit * (grid_size // 2)) % grid_size
    for bit_pos in range((grid_size - 1).bit_length()):
        shifted = shifted_2(operand, "col", -(2 << bit_pos))
        operand = jnp.where((steps_wanted >> bit_pos) % 2 == 1, shifted, operand)
    return operand


def skew_right(operand, tile_col, layer_bit, grid_size):
    steps_wanted = (tile_col + layer_bit * (grid_size // 2)) % grid_size
    for bit_pos in range((grid_size - 1).bit_length()):
        shifted = shifted_2(operand, "row", -(1 << bit_pos))
        operand = jnp.where((steps_wanted >> bit_pos) % 2 == 1, shifted, operand)
    return operand


def cannon_half(left, right, grid_size):
    running = jnp.zeros((left.shape[0], right.shape[1]), jnp.float32)
    for section in range(grid_size // 2):
        running = running + jnp.dot(left, right, preferred_element_type=jnp.float32)
        if section + 1 < grid_size // 2:
            left = shifted_2(left, "col", -2)
            right = shifted_2(right, "row", -1)
    return running


def per_device_ring(upper_stored, block_cells):
    grid_size = lax.axis_size("row")
    row_id = lax.axis_index("row")
    col_id = lax.axis_index("col")
    layer_bit = col_id % 2
    tile_col = col_id // 2
    tile_side, half_width = upper_stored.shape
    order_total = tile_side * grid_size
    tile_blocks = tile_side // BLK
    half_blocks = half_width // BLK
    slab_width = half_width // grid_size
    stacked = lax.all_to_all(
        lax.all_to_all(upper_stored, "row", split_axis=1, concat_axis=0, tiled=True),
        "col",
        split_axis=0,
        concat_axis=1,
        tiled=True,
    )
    gathered = lax.all_to_all(stacked.T, "row", split_axis=0, concat_axis=0, tiled=True)
    mirrored = (
        gathered.reshape(grid_size, 2, slab_width, half_width)
        .transpose(1, 0, 2, 3)
        .reshape(tile_side, half_width)
    )
    global_rows = row_id * tile_side + lax.broadcasted_iota(jnp.int32, (tile_side, half_width), 0)
    global_cols = col_id * half_width + lax.broadcasted_iota(jnp.int32, (tile_side, half_width), 1)
    symmetric = jnp.where(global_rows <= global_cols, upper_stored, mirrored)
    near_own = cell_mask(
        block_cells, row_id * tile_blocks, tile_blocks, col_id * half_blocks, half_blocks, NEAR
    )
    diagonal = jnp.where(global_rows == global_cols, 0.5, 0.0).astype(jnp.float32)
    value_scale = 2.0 / math.sqrt(order_total)
    own_density = block_keep(
        diagonal + value_scale * symmetric.astype(jnp.float32), near_own
    ).astype(jnp.bfloat16)
    partner_density = partner(own_density, "col", 0)
    density = join_halves(own_density, partner_density, layer_bit)
    right_start = skew_right(density, tile_col, layer_bit, grid_size)
    left_start = skew_left(density, row_id, layer_bit, grid_size)
    running = cannon_half(left_start, right_start, grid_size)
    far_full = cell_mask(
        block_cells, row_id * tile_blocks, tile_blocks, tile_col * tile_blocks, tile_blocks, FAR
    )
    partner_running = partner(running, "col", 0)
    square = block_keep(running + partner_running, far_full)
    square_low = square.astype(jnp.bfloat16)
    own_square = own_part(square, layer_bit, half_width)
    right_again = skew_right(density, tile_col, layer_bit, grid_size)
    left_again = skew_left(square_low, row_id, layer_bit, grid_size)
    cubic_running = cannon_half(left_again, right_again, grid_size)
    received_cubic = partner(partner_part(cubic_running, layer_bit, half_width), "col", 0)
    cubic = own_part(cubic_running, layer_bit, half_width) + received_cubic
    return block_keep(3.0 * own_square - 2.0 * cubic, near_own).astype(jnp.bfloat16)


def wrapped_square(row_cells, col_cells):
    total = 0
    for axis in range(3):
        offset = jnp.abs(row_cells[axis] - col_cells[axis])
        wrapped = jnp.minimum(offset, BOX - offset)
        total = total + wrapped * wrapped
    return total


def masked_density(upper_stored, block_cells):
    rows, cols = upper_stored.shape
    row_start = lax.axis_index("row") * rows
    col_start = lax.axis_index("col") * cols
    order_total = rows * lax.axis_size("row")
    row_cells = lax.dynamic_slice_in_dim(block_cells, row_start // BLK, rows // BLK, 0)
    col_cells = lax.dynamic_slice_in_dim(block_cells, col_start // BLK, cols // BLK, 0)
    row_cells = jnp.repeat(row_cells, BLK, axis=0)
    col_cells = jnp.repeat(col_cells, BLK, axis=0)
    near = wrapped_square(
        [row_cells[:, a][:, None] for a in range(3)], [col_cells[:, a][None, :] for a in range(3)]
    )
    global_rows = row_start + lax.broadcasted_iota(jnp.int32, (rows, cols), 0)
    global_cols = col_start + lax.broadcasted_iota(jnp.int32, (rows, cols), 1)
    diagonal = jnp.where(global_rows == global_cols, 0.5, 0.0).astype(jnp.float32)
    value = diagonal + (2.0 / math.sqrt(order_total)) * upper_stored.astype(jnp.float32)
    return jnp.where(near <= NEAR, value, 0.0).astype(jnp.bfloat16)


def purify_kernel(cells_ref, lanes_ref, blocks_ref, out_ref, density, square_low, own, sems):
    rows, cols = out_ref.shape
    order_total = density.shape[0]
    columns = order_total // cols
    per_row = rows // cols
    row_id = lax.axis_index("row")
    col_id = lax.axis_index("col")

    def load(i, j):
        return pltpu.make_async_copy(
            blocks_ref.at[(i // per_row) * columns + j, pl.ds((i % per_row) * cols, cols)],
            density.at[pl.ds(i * cols, cols), pl.ds(j * cols, cols)],
            sems.at[i * columns + j],
        )

    pairs = [(i, j) for j in range(columns) for i in range(j + 1)]
    for i, j in pairs:
        load(i, j).start()
    below = lax.broadcasted_iota(jnp.int32, (cols, cols), 0) > lax.broadcasted_iota(
        jnp.int32, (cols, cols), 1
    )
    for i, j in pairs:
        load(i, j).wait()
        upper = density[i * cols : (i + 1) * cols, j * cols : (j + 1) * cols]
        flipped = upper.T
        if i == j:
            flipped = jnp.where(below, flipped, upper)
        density[j * cols : (j + 1) * cols, i * cols : (i + 1) * cols] = flipped

    def keep(value, lanes, bound):
        pieces = []
        for block in range(rows // BLK):
            row = row_id * (rows // BLK) + block
            distance = wrapped_square(
                [cells_ref[row, a] for a in range(3)], [lanes[a : a + 1, :] for a in range(3)]
            )
            piece = value[block * BLK : (block + 1) * BLK]
            pieces.append(jnp.where(distance <= bound, piece, 0.0))
        return jnp.concatenate(pieces, 0)

    own_rows = pl.ds(pl.multiple_of(row_id * rows, rows), rows)

    @pl.loop(0, columns)
    def _(j):
        here = pl.ds(pl.multiple_of(j * cols, cols), cols)
        product = jnp.dot(
            density[own_rows, :], density[:, here], preferred_element_type=jnp.float32
        )
        square = keep(product, lanes_ref[:, here], FAR)
        square_low[:, here] = square.astype(jnp.bfloat16)

        @pl.when(j == col_id)
        def _():
            own[...] = square

    mine = pl.ds(pl.multiple_of(col_id * cols, cols), cols)
    cubic = jnp.dot(square_low[...], density[:, mine], preferred_element_type=jnp.float32)
    result = 3.0 * own[...] - 2.0 * cubic
    out_ref[...] = keep(result, lanes_ref[:, mine], NEAR).astype(jnp.bfloat16)


def gather_kernel(
    own_ref, blocks_ref, z_send, z_recv, p_send, p_recv, d_send, d_recv, c_send, c_recv, local_sem
):
    rows = own_ref.shape[0]
    half = rows // 2
    columns = lax.axis_size("col")
    layers = columns // 2
    row_id = lax.axis_index("row")
    col_id = lax.axis_index("col")
    z, core = col_id // 2, col_id % 2
    x_row = row_id + 1 - 2 * (row_id % 2)
    y_row = (row_id + 2) % 4
    diag_row = (x_row + 2) % 4
    mesh_id = pl.DeviceIdType.MESH
    to_x, to_y = (x_row, col_id), (y_row, col_id)
    to_core = (row_id, col_id + 1 - 2 * core)
    up, down = (row_id, col_id + 2), (row_id, col_id - 2)
    has_up, has_down = z + 1 < layers, z > 0

    barrier = pltpu.get_barrier_semaphore()
    for target in (to_x, to_y, to_core):
        pl.semaphore_signal(barrier, inc=1, device_id=target, device_id_type=mesh_id)

    @pl.when(has_up)
    def _():
        pl.semaphore_signal(barrier, inc=1, device_id=up, device_id_type=mesh_id)

    @pl.when(has_down)
    def _():
        pl.semaphore_signal(barrier, inc=1, device_id=down, device_id_type=mesh_id)

    pl.semaphore_wait(barrier, 3 + has_up.astype(jnp.int32) + has_down.astype(jnp.int32))

    far_slot = layers - 1
    slots = [0]
    for step in range(far_slot):
        slots += [1 + step, 1 + far_slot + step]

    def layer(slot):
        if slot == 0:
            return z
        if slot <= far_slot:
            return z - slot
        return z + slot - far_slot

    def valid(slot, act):
        if slot == 0:
            act()
        elif slot <= far_slot:
            pl.when(z >= slot)(act)
        else:
            pl.when(z + slot - far_slot < layers)(act)

    def used(row, slot, act):
        pl.when(row * rows < (2 * layer(slot) + 2) * own_ref.shape[1])(act)

    def part(row, slot, piece):
        index = row * columns + 2 * layer(slot) + core
        block = blocks_ref.at[index]
        return block if piece is None else block.at[pl.ds(piece * half, half)]

    def copy(row, slot, piece, target, send, recv, first=False):
        place = part(row, slot, piece)
        return pltpu.make_async_remote_copy(
            src_ref=own_ref if first else place,
            dst_ref=place,
            send_sem=send,
            recv_sem=recv,
            device_id=target,
            device_id_type=mesh_id,
        )

    def z_up(slot):
        return copy(row_id, slot, None, up, z_send.at[slot, 0], z_recv.at[slot + 1], slot == 0)

    def z_down(slot):
        later = 1 + far_slot if slot == 0 else slot + 1
        return copy(row_id, slot, None, down, z_send.at[slot, 1], z_recv.at[later], slot == 0)

    def goes_up(slot):
        return slot < far_slot

    def goes_down(slot):
        return slot == 0 or far_slot < slot < 2 * far_slot

    def plane(slot, way):
        return copy(
            row_id, slot, None, (to_x, to_y)[way], p_send.at[slot, way], p_recv.at[slot, way], slot == 0
        )

    def relay(slot, way):
        row = (x_row, y_row)[way]
        target = (to_y, to_x)[way]
        return copy(row, slot, way, target, d_send.at[slot, way], d_recv.at[slot, way])

    def across(slot, kind):
        row = (row_id, x_row, y_row, diag_row, diag_row)[kind]
        piece = (None, None, None, 0, 1)[kind]
        return copy(
            row, slot, piece, to_core, c_send.at[slot, kind], c_recv.at[slot, kind],
            slot == 0 and kind == 0,
        )

    def stage_own(slot):
        def act():
            if slot:
                copy(row_id, slot, None, up, z_send.at[slot, 0], z_recv.at[slot]).wait_recv()
            if goes_up(slot):
                pl.when(has_up)(lambda: z_up(slot).start())
            if goes_down(slot):
                pl.when(has_down)(lambda: z_down(slot).start())
            plane(slot, 0).start()
            plane(slot, 1).start()
            across(slot, 0).start()

        valid(slot, lambda: used(row_id, slot, act))

    def stage_relay(slot):
        def one(way):
            plane_in = (x_row, y_row)[way]
            copy(
                plane_in, slot, None, to_x, p_send.at[slot, way], p_recv.at[slot, way]
            ).wait_recv()
            relay(slot, way).start()
            across(slot, 1 + way).start()

        def act():
            used(x_row, slot, lambda: one(0))
            used(y_row, slot, lambda: one(1))

        valid(slot, act)

    def stage_diag(slot):
        def act():
            for way in range(2):
                copy(
                    diag_row, slot, way, to_x, d_send.at[slot, way], d_recv.at[slot, way]
                ).wait_recv()
                across(slot, 3 + way).start()

        valid(slot, lambda: used(diag_row, slot, act))

    def stage_end(slot):
        def own_end():
            if goes_up(slot):
                pl.when(has_up)(lambda: z_up(slot).wait_send())
            if goes_down(slot):
                pl.when(has_down)(lambda: z_down(slot).wait_send())
            for way in range(2):
                plane(slot, way).wait_send()
            across(slot, 0).wait()

        def relay_end(way):
            relay(slot, way).wait_send()
            across(slot, 1 + way).wait()

        def diag_end():
            across(slot, 3).wait()
            across(slot, 4).wait()

        def act():
            used(row_id, slot, own_end)
            used(x_row, slot, lambda: relay_end(0))
            used(y_row, slot, lambda: relay_end(1))
            used(diag_row, slot, diag_end)

        valid(slot, act)

    keep_own = pltpu.make_async_copy(own_ref, part(row_id, 0, None), local_sem)
    keep_own.start()
    groups = [[0]] + [[1 + step, 1 + far_slot + step] for step in range(far_slot)]
    for turn in range(len(groups) + 2):
        for lag, stage in enumerate((stage_own, stage_relay, stage_diag)):
            if 0 <= turn - lag < len(groups):
                for slot in groups[turn - lag]:
                    stage(slot)
    for slot in slots:
        stage_end(slot)
    keep_own.wait()


def gather_blocks(own):
    rows, cols = own.shape
    columns = lax.axis_size("col")
    count = lax.axis_size("row") * columns
    slots = columns - 1
    dma = pltpu.SemaphoreType.DMA
    anywhere = pl.BlockSpec(memory_space=pl.ANY)
    return pl.pallas_call(
        gather_kernel,
        out_shape=jax.ShapeDtypeStruct((count, rows, cols), own.dtype),
        in_specs=[anywhere],
        out_specs=anywhere,
        scratch_shapes=[
            dma((slots, 2)), dma((slots,)),
            dma((slots, 2)), dma((slots, 2)),
            dma((slots, 2)), dma((slots, 2)),
            dma((slots, 5)), dma((slots, 5)),
            dma,
        ],
        compiler_params=pltpu.CompilerParams(collective_id=0, has_side_effects=True),
    )(own)


def per_device_gather(upper_stored, block_cells):
    rows, cols = upper_stored.shape
    order_total = rows * lax.axis_size("row")
    columns = order_total // cols
    blocks = gather_blocks(masked_density(upper_stored, block_cells))
    lanes = jnp.zeros((8, order_total), jnp.int32).at[:3].set(jnp.repeat(block_cells, BLK, axis=0).T)
    vmem = pl.BlockSpec(memory_space=pltpu.VMEM)
    return pl.pallas_call(
        purify_kernel,
        out_shape=jax.ShapeDtypeStruct((rows, cols), jnp.bfloat16),
        in_specs=[
            pl.BlockSpec(memory_space=pltpu.SMEM),
            vmem,
            pl.BlockSpec(memory_space=pl.ANY),
        ],
        out_specs=vmem,
        scratch_shapes=[
            pltpu.VMEM((order_total, order_total), jnp.bfloat16),
            pltpu.VMEM((rows, order_total), jnp.bfloat16),
            pltpu.VMEM((rows, cols), jnp.float32),
            pltpu.SemaphoreType.DMA((columns * columns,)),
        ],
        compiler_params=pltpu.CompilerParams(vmem_limit_bytes=48 * 2**20),
    )(block_cells, lanes, blocks)


def per_device(upper_stored, block_cells):
    order_total = upper_stored.shape[0] * lax.axis_size("row")
    if lax.axis_size("row") != 4 or order_total * order_total * 2 > 24 * 2**20:
        return per_device_ring(upper_stored, block_cells)
    return per_device_gather(upper_stored, block_cells)


def solution(mesh):
    return jax.shard_map(
        per_device,
        mesh=mesh,
        in_specs=(P("row", "col"), P()),
        out_specs=P("row", "col"),
        check_vma=False,
    )
```
